32 devices in a mesh: groups: 2 (over x), tile: 16 (over z, y, core).
Axes of the slice: x: 2, y: 2, z: 4, core: 2. Of those that a mesh axis runs over, the one named last changes fastest.
Arguments:
- pair_tiles: bfloat16 [32, 64, 64, 128], P(('groups', 'tile')), parts along dimension 0, may hold values from -6 to 6
- cotangent: bfloat16 [32, 64, 64, 128], P(('groups', 'tile')), parts along dimension 0, may hold values from -6 to 6
- w_pair: bfloat16 [2, 128, 512], replicated, may hold values from -0.5 to 0.5
- w_gate: bfloat16 [2, 128, 128], replicated, may hold values from -0.5 to 0.5
- w_out: bfloat16 [2, 128, 128], replicated, may hold values from -0.5 to 0.5
- tile_lists: int32 [2, 32, 2, 2], P(None, 'groups'), parts along dimension 1, may hold values from 0 to 15
- list_counts: int32 [2, 32], P(None, 'groups'), parts along dimension 1, may hold values from 1 to 2
Outputs:
- new_pair: bfloat16 [32, 64, 64, 128], P(('groups', 'tile')), parts along dimension 0
- d_pair: bfloat16 [32, 64, 64, 128], P(('groups', 'tile')), parts along dimension 0
- grad_pair: float32 [4, 128, 512], P('groups', 'tile'), parts along dimension 0
- grad_gate: float32 [4, 128, 128], P('groups', 'tile'), parts along dimension 0
- grad_out: float32 [4, 128, 128], P('groups', 'tile'), parts along dimension 0
The draws below stay inside these ranges and needn't reach their ends.
There are 2 independent parts, one for each index of `groups`. The reference program is written for one: setup_inputs(seed, part) draws one part's arguments, and reference() takes and returns one part's arrays. A program takes and returns all parts, laid end to end along the dimension named above; an argument that names none is the same for every part. Nothing has to cross between parts.
Inputs may be any that keep to these rules, and one draw needn't show every extreme that they name: `tile_lists`: each slot names two kept tiles by their index in the tile order; slots from list_counts on are unused.
All inputs are finite; a program needn't handle non-finite values.
Results may differ from the reference program's by a relative error of at most 0.015.
Values may be sent and summed in bfloat16 or wider, within the bound.
A program may use at most 192 MiB of HBM per device.

```python
import math
import jax
import jax.numpy as jnp
from jax import lax

C = 128
B = 64
KMAX = 2
TILES = 16


def place_ends(entries, rng, smallest, largest):
    spot = [jax.random.randint(jax.random.fold_in(rng, axis), (), 0, length) for axis, length in enumerate(entries.shape)]
    longest = entries.shape.index(max(entries.shape))
    next_to = spot[:longest] + [(spot[longest] + 1) % entries.shape[longest]] + spot[longest + 1:]
    return entries.at[tuple(spot)].set(smallest).at[tuple(next_to)].set(largest)


def levels(own_key, shape, cuts, low, largest):
    def one(dim, shards_of):
        draws = jax.random.uniform(jax.random.fold_in(jax.random.fold_in(own_key, 6), dim), (shards_of,), jnp.float32, low / len(cuts), largest / len(cuts))
        return jnp.repeat(jnp.exp(draws), shape[dim] // shards_of).reshape((-1,) + (1,) * (len(shape) - dim - 1))

    level = one(*cuts[0])
    for cut in cuts[1:]:
        level = level * one(*cut)
    return level


def normal_values(own_key, shape, scale, bound, split=(), kind=jnp.bfloat16):
    entries = scale * jax.random.normal(own_key, shape, jnp.float32)
    if split:
        entries = entries * levels(own_key, shape, split, -0.22, 0.18)
    return jnp.clip(entries, -bound, bound).astype(kind)


def setup_inputs(seed: int = 0, part: int = 0) -> dict:
    key_list = jax.random.split(jax.random.key(seed), 8)
    own_keys = jax.random.split(jax.random.fold_in(key_list[7], part), 8)
    return {
        "pair_tiles": normal_values(own_keys[0], (TILES, B, B, C), 1.0, 6.0, ((0, 16),)),
        "cotangent": normal_values(own_keys[1], (TILES, B, B, C), 1.0, 6.0, ((0, 16),)),
        "w_pair": normal_values(key_list[2], (2, C, 4 * C), C ** -0.5, 0.5),
        "w_gate": normal_values(key_list[3], (2, C, C), C ** -0.5, 0.5),
        "w_out": normal_values(key_list[4], (2, C, C), C ** -0.5, 0.5),
        "tile_lists": place_ends(jax.random.randint(own_keys[5], (2, TILES, KMAX, 2), 0, TILES), jax.random.fold_in(own_keys[5], 1), 0, TILES - 1).astype(jnp.int32),
        "list_counts": place_ends(jax.random.randint(own_keys[6], (2, TILES), 1, KMAX + 1), jax.random.fold_in(own_keys[6], 1), 1, KMAX).astype(jnp.int32),
    }


EPS = 1e-05

def mixed_product(pattern, one_side, other_side):
    return jnp.einsum(pattern, one_side.astype(jnp.float32), other_side.astype(jnp.float32))

def normalize(values, axis_index):
    center = lax.optimization_barrier(jnp.mean(values, axis=axis_index, keepdims=True))
    shifted = values - center
    spread = lax.optimization_barrier(jnp.mean(shifted * shifted, axis=axis_index, keepdims=True))
    factor = lax.rsqrt(spread + EPS)
    return (shifted * factor, factor)

def norm_back(upstream, normed, factor, axis_index):
    first_mean = lax.optimization_barrier(jnp.mean(upstream, axis=axis_index, keepdims=True))
    cross_mean = lax.optimization_barrier(jnp.mean(upstream * normed, axis=axis_index, keepdims=True))
    return factor * (upstream - first_mean - normed * cross_mean)

def project_in(pair_tiles, w_pair, w_gate):
    normed, in_factor = normalize(pair_tiles.astype(jnp.float32), 3)
    normed_low = normed.astype(jnp.bfloat16)
    projected = mixed_product('tijd,de->teij', normed_low, w_pair)
    channels = w_gate.shape[0]
    left_side = (projected[:, :channels] * jax.nn.sigmoid(projected[:, channels:2 * channels])).astype(jnp.bfloat16)
    right_side = (projected[:, 2 * channels:3 * channels] * jax.nn.sigmoid(projected[:, 3 * channels:])).astype(jnp.bfloat16)
    out_gate = jax.nn.sigmoid(mixed_product('tijd,de->tije', normed_low, w_gate))
    return (left_side, right_side, (normed, in_factor, normed_low, out_gate))

def project_out(pair_tiles, product, out_gate, w_out):
    normed, out_factor = normalize(product.astype(jnp.float32), 1)
    normed_low = normed.astype(jnp.bfloat16)
    update = mixed_product('tcij,ce->tije', normed_low, w_out)
    new_pair = (pair_tiles.astype(jnp.float32) + out_gate * update).astype(jnp.bfloat16)
    return (new_pair, (normed, out_factor, normed_low, update))

def triangle(left_chan, right_chan, slot_lists, amounts, incoming):
    pattern = 'tcki,tckj->tcij' if incoming else 'tcik,tcjk->tcij'

    def accumulate(column, summed):
        alive_mask = (column < amounts).astype(left_chan.dtype)[:, None, None, None]
        left_live = jnp.take(left_chan, slot_lists[:, column, 0], axis=0) * alive_mask
        right_rows = jnp.take(right_chan, slot_lists[:, column, 1], axis=0)
        return summed + mixed_product(pattern, left_live, right_rows)
    initial = jnp.zeros(left_chan.shape, jnp.float32)
    summed = lax.fori_loop(0, slot_lists.shape[1], accumulate, initial)
    return summed.astype(jnp.bfloat16)

def triangle_back(left_chan, right_chan, slot_lists, amounts, incoming, upstream):
    left_form = 'tckj,tcij->tcki' if incoming else 'tcjk,tcij->tcik'
    right_form = 'tcki,tcij->tckj' if incoming else 'tcik,tcij->tcjk'

    def accumulate(column, totals):
        left_index = slot_lists[:, column, 0]
        right_index = slot_lists[:, column, 1]
        alive_mask = (column < amounts).astype(left_chan.dtype)[:, None, None, None]
        left_live = jnp.take(left_chan, left_index, axis=0) * alive_mask
        right_live = jnp.take(right_chan, right_index, axis=0) * alive_mask
        left_grad = mixed_product(left_form, right_live, upstream)
        right_grad = mixed_product(right_form, left_live, upstream)
        return (totals[0].at[left_index].add(left_grad), totals[1].at[right_index].add(right_grad))
    initial = jnp.zeros(left_chan.shape, jnp.float32)
    left_total, right_total = lax.fori_loop(0, slot_lists.shape[1], accumulate, (initial, initial))
    return (left_total.astype(jnp.bfloat16), right_total.astype(jnp.bfloat16))

def back_out(upstream, out_saved, out_gate, w_out):
    normed, out_factor, normed_low, update = out_saved
    grad_update = (upstream * out_gate).astype(jnp.bfloat16)
    grad_logit = (upstream * update * out_gate * (1.0 - out_gate)).astype(jnp.bfloat16)
    grad_wout = mixed_product('tcij,tije->ce', normed_low, grad_update)
    grad_normed = mixed_product('tije,ce->tcij', grad_update, w_out)
    grad_product = norm_back(grad_normed, normed, out_factor, 1).astype(jnp.bfloat16)
    return (grad_product, grad_logit, grad_wout)

def back_in(residual_grad, grad_left, grad_right, grad_logit, in_saved, w_pair, w_gate):
    normed, in_factor, normed_low, out_gate = in_saved
    channels = w_gate.shape[0]
    projected = mixed_product('tijd,de->teij', normed_low, w_pair)
    left_val = projected[:, :channels]
    left_sig = jax.nn.sigmoid(projected[:, channels:2 * channels])
    right_val = projected[:, 2 * channels:3 * channels]
    right_sig = jax.nn.sigmoid(projected[:, 3 * channels:])
    left_flow = grad_left.astype(jnp.float32)
    right_flow = grad_right.astype(jnp.float32)
    grad_proj = jnp.concatenate([left_flow * left_sig, left_flow * left_val * left_sig * (1.0 - left_sig), right_flow * right_sig, right_flow * right_val * right_sig * (1.0 - right_sig)], axis=1).astype(jnp.bfloat16)
    grad_wpair = mixed_product('tijd,teij->de', normed_low, grad_proj)
    grad_wgate = mixed_product('tijd,tije->de', normed_low, grad_logit)
    grad_normed = mixed_product('teij,de->tijd', grad_proj, w_pair) + mixed_product('tije,de->tijd', grad_logit, w_gate)
    return (residual_grad + norm_back(grad_normed, normed, in_factor, 3), grad_wpair, grad_wgate)

def forward_module(pair_tiles, w_pair, w_gate, w_out, slot_lists, amounts, incoming):
    left_side, right_side, in_saved = project_in(pair_tiles, w_pair, w_gate)
    product = triangle(left_side, right_side, slot_lists, amounts, incoming)
    new_pair, out_saved = project_out(pair_tiles, product, in_saved[3], w_out)
    return (new_pair, (left_side, right_side, in_saved, out_saved))

def backward_module(upstream, states, w_pair, w_gate, w_out, slot_lists, amounts, incoming):
    left_side, right_side, in_saved, out_saved = states
    grad_product, grad_logit, grad_wout = back_out(upstream, out_saved, in_saved[3], w_out)
    grad_left, grad_right = triangle_back(left_side, right_side, slot_lists, amounts, incoming, grad_product)
    grad_input, grad_wpair, grad_wgate = back_in(upstream, grad_left, grad_right, grad_logit, in_saved, w_pair, w_gate)
    return (grad_input, (grad_wpair, grad_wgate, grad_wout))

def reference(pair_tiles, cotangent, w_pair, w_gate, w_out, tile_lists, list_counts):
    current = pair_tiles
    saved_list = []
    for layer_index in range(2):
        current, states = forward_module(current, w_pair[layer_index], w_gate[layer_index], w_out[layer_index], tile_lists[layer_index], list_counts[layer_index], layer_index == 1)
        saved_list.append(states)
    new_pair = current
    upstream = cotangent.astype(jnp.float32)
    collected = [None, None]
    for layer_index in (1, 0):
        upstream, weight_grads = backward_module(upstream, saved_list[layer_index], w_pair[layer_index], w_gate[layer_index], w_out[layer_index], tile_lists[layer_index], list_counts[layer_index], layer_index == 1)
        collected[layer_index] = weight_grads
    cell_scale = 1.0 / math.sqrt(TILES * B * B)
    grad_pair = jnp.stack([collected[0][0], collected[1][0]]) * cell_scale
    grad_gate = jnp.stack([collected[0][1], collected[1][1]]) * cell_scale
    grad_out = jnp.stack([collected[0][2], collected[1][2]]) * cell_scale
    return (new_pair, upstream.astype(jnp.bfloat16), grad_pair, grad_gate, grad_out)
```

```python
import functools
import math

import jax
import jax.numpy as jnp
from jax import lax
from jax.experimental import pallas as pl
from jax.experimental.pallas import tpu as pltpu
from jax.sharding import PartitionSpec as P

EPS = 1e-05
CHUNK = 512
VMEM_BYTES = 40 * 1024 * 1024
F32, BF16 = jnp.float32, jnp.bfloat16


def dot(one, other, one_dim, other_dim):
    return lax.dot_general(one, other, (((one_dim,), (other_dim,)), ((), ())), preferred_element_type=F32)


def sigmoid(values):
    return 0.5 * jnp.tanh(0.5 * values) + 0.5


def normalize(values):
    shifted = values - jnp.mean(values, axis=0, keepdims=True)
    factor = lax.rsqrt(jnp.mean(shifted * shifted, axis=0, keepdims=True) + EPS)
    return shifted * factor, factor


def norm_back(upstream, normed, factor):
    first_mean = jnp.mean(upstream, axis=0, keepdims=True)
    cross_mean = jnp.mean(upstream * normed, axis=0, keepdims=True)
    return factor * (upstream - first_mean - normed * cross_mean)


def gated(normed_low, w_val, w_sig):
    return dot(w_val, normed_low, 1, 0), sigmoid(dot(w_sig, normed_low, 1, 0))


def project_in(pair, w_val, w_sig, lr_ref):
    normed_low = normalize(pair)[0].astype(BF16)
    value, sig = gated(normed_low, w_val[...], w_sig[...])
    lr_ref[...] = (value * sig).astype(BF16)


def out_parts(pair, prod_ref, w_gate, w_out):
    in_low = normalize(pair)[0].astype(BF16)
    gate = sigmoid(dot(w_gate[...], in_low, 0, 0))
    normed, factor = normalize(prod_ref[...].astype(F32))
    normed_low = normed.astype(BF16)
    update = dot(w_out[...], normed_low, 0, 0)
    return in_low, gate, normed, factor, normed_low, update


def accumulate(ref, value):
    @pl.when(pl.program_id(0) == 0)
    def _():
        ref[...] = jnp.zeros_like(ref)

    ref[...] += value


def back_out(upstream, parts, w_out, gprod_ref, glogit_ref, dgate_ref, dout_ref):
    in_low, gate, normed, factor, normed_low, update = parts
    grad_update = (upstream * gate).astype(BF16)
    grad_logit = (upstream * update * gate * (1.0 - gate)).astype(BF16)
    glogit_ref[...] = grad_logit
    accumulate(dout_ref, dot(normed_low, grad_update, 1, 1))
    accumulate(dgate_ref, dot(in_low, grad_logit, 1, 1))
    grad_normed = dot(w_out[...], grad_update, 1, 0)
    gprod_ref[...] = norm_back(grad_normed, normed, factor).astype(BF16)


def back_in(upstream, pair, glr_ref, glogit_ref, w_val, w_sig, w_gate, dpair_ref):
    normed, factor = normalize(pair)
    normed_low = normed.astype(BF16)
    value, sig = gated(normed_low, w_val[...], w_sig[...])
    flow = glr_ref[...].astype(F32)
    grad_val = flow * sig
    grad_sig = (grad_val * value * (1.0 - sig)).astype(BF16)
    grad_val = grad_val.astype(BF16)
    rows = grad_val.shape[0]
    accumulate(dpair_ref.at[:, :rows], dot(normed_low, grad_val, 1, 1))
    accumulate(dpair_ref.at[:, rows:], dot(normed_low, grad_sig, 1, 1))
    grad_normed = (
        dot(w_val[...], grad_val, 0, 0)
        + dot(w_sig[...], grad_sig, 0, 0)
        + dot(w_gate[...], glogit_ref[...], 1, 0)
    )
    return upstream + norm_back(grad_normed, normed, factor)


def turned(ref):
    return ref[...].astype(F32).T


def first_kernel(x_ref, wv, ws, lr_ref):
    project_in(turned(x_ref), wv, ws, lr_ref)


def middle_kernel(x_ref, prod_ref, wgate, wout, wv, ws, pair_ref, lr_ref):
    pair = turned(x_ref)
    _, gate, _, _, _, update = out_parts(pair, prod_ref, wgate, wout)
    low = (pair + gate * update).astype(BF16)
    pair_ref[...] = low
    project_in(low.astype(F32), wv, ws, lr_ref)


def top_kernel(pair_ref, prod_ref, cot_ref, wgate, wout, new_ref, gprod_ref, glogit_ref, dgate_ref, dout_ref):
    pair = pair_ref[...].astype(F32)
    parts = out_parts(pair, prod_ref, wgate, wout)
    new_ref[...] = (pair + parts[1] * parts[5]).T.astype(BF16)
    back_out(turned(cot_ref), parts, wout, gprod_ref, glogit_ref, dgate_ref, dout_ref)


def turn_kernel(
    pair_ref, cot_ref, glr_ref, glogit1_ref, x_ref, prod_ref, wv1, ws1, wgate1, wgate0, wout0,
    up_ref, gprod_ref, glogit_ref, dpair_ref, dgate_ref, dout_ref,
):
    upstream = back_in(
        turned(cot_ref), pair_ref[...].astype(F32), glr_ref, glogit1_ref, wv1, ws1, wgate1, dpair_ref
    )
    up_ref[...] = upstream
    parts = out_parts(turned(x_ref), prod_ref, wgate0, wout0)
    back_out(upstream, parts, wout0, gprod_ref, glogit_ref, dgate_ref, dout_ref)


def last_kernel(x_ref, up_ref, glr_ref, glogit_ref, wv, ws, wgate, dx_ref, dpair_ref):
    grad = back_in(up_ref[...], turned(x_ref), glr_ref, glogit_ref, wv, ws, wgate, dpair_ref)
    dx_ref[...] = grad.T.astype(BF16)


def cellwise(kernel, name, args, outs, cells):
    step = min(CHUNK, cells)

    def spec(kind, shape):
        if kind == "r":
            return pl.BlockSpec((step, shape[1]), lambda n: (n, 0))
        if kind == "c":
            return pl.BlockSpec((shape[0], step), lambda n: (0, n))
        return pl.BlockSpec(shape, lambda n: (0, 0))

    return pl.pallas_call(
        kernel,
        name=name,
        grid=(cells // step,),
        in_specs=[spec(kind, array.shape) for kind, array in args],
        out_specs=[spec(kind, shape) for kind, shape, _ in outs],
        out_shape=[jax.ShapeDtypeStruct(shape, kind) for _, shape, kind in outs],
        compiler_params=pltpu.CompilerParams(vmem_limit_bytes=VMEM_BYTES),
    )(*[array for _, array in args])


def triangle_kernel(incoming, tiles, kmax, chans, lists, counts, lr_ref, prod_ref):
    dim = 0 if incoming else 1

    def one(tile, _):
        def term(slot, chan):
            base = (tile * kmax + slot) * 2
            return dot(lr_ref[lists[base], chan], lr_ref[lists[base + 1], chans + chan], dim, dim)

        used = counts[tile]
        for chan in range(chans):
            total = term(0, chan)
            for slot in range(1, kmax):
                total = total + jnp.where(slot < used, term(slot, chan), 0.0)
            prod_ref[tile, chan] = total.astype(BF16)
        return 0

    lax.fori_loop(0, tiles, one, 0)


def triangle_back_kernel(incoming, tiles, kmax, chans, lists, counts, lr_ref, gprod_ref, glr_ref, total):
    total[...] = jnp.zeros_like(total)

    def one(tile, _):
        for slot in range(kmax):

            @pl.when(slot < counts[tile])
            def _():
                base = (tile * kmax + slot) * 2
                x, y = lists[base], lists[base + 1]
                for chan in range(chans):
                    grad = gprod_ref[tile, chan]
                    left, right = lr_ref[x, chan], lr_ref[y, chans + chan]
                    if incoming:
                        total[x, chan] += dot(right, grad, 1, 1)
                        total[y, chans + chan] += dot(left, grad, 1, 0)
                    else:
                        total[x, chan] += dot(grad, right, 1, 0)
                        total[y, chans + chan] += dot(grad, left, 0, 0)
        return 0

    lax.fori_loop(0, tiles, one, 0)

    def store(tile, _):
        glr_ref[tile] = total[tile].astype(BF16)
        return 0

    lax.fori_loop(0, tiles, store, 0)


def tile_call(kernel, name, scalars, arrays, out_shape, scratch):
    return pl.pallas_call(
        kernel,
        name=name,
        in_specs=[pl.BlockSpec(memory_space=pltpu.SMEM)] * len(scalars)
        + [pl.BlockSpec(memory_space=pltpu.VMEM)] * len(arrays),
        out_specs=pl.BlockSpec(memory_space=pltpu.VMEM),
        out_shape=jax.ShapeDtypeStruct(out_shape, BF16),
        scratch_shapes=scratch,
        compiler_params=pltpu.CompilerParams(vmem_limit_bytes=VMEM_BYTES),
    )(*scalars, *arrays)


def exchange(array):
    return lax.all_to_all(array, "tile", split_axis=0, concat_axis=0, tiled=True)


def local(devices, pair_tiles, cotangent, w_pair, w_gate, w_out, tile_lists, list_counts):
    owned, side, _, channels = pair_tiles.shape
    cells = owned * side * side
    tiles, kmax = tile_lists.shape[1], tile_lists.shape[2]
    chans = channels // devices
    x = pair_tiles.reshape(cells, channels)
    cot = cotangent.reshape(cells, channels)
    weights = w_pair.reshape(2, channels, 2, 2, devices, chans)
    weights = weights.transpose(0, 3, 4, 2, 5, 1).reshape(2, 2, 2 * channels, channels)
    wide = 2 * channels
    col, row = "c", "r"

    def lists(m):
        return tile_lists[m].reshape(-1), list_counts[m]

    def triangle(lr, m):
        lr = exchange(lr.reshape(devices, 2 * chans, cells)).reshape(tiles, 2 * chans, side, side)
        kernel = functools.partial(triangle_kernel, m == 1, tiles, kmax, chans)
        prod = tile_call(kernel, f"triangle{m}", lists(m), (lr,), (tiles, chans, side, side), [])
        return lr, exchange(prod.reshape(tiles, chans, cells)).reshape(channels, cells)

    def triangle_back(lr, gprod, m):
        gprod = exchange(gprod.reshape(devices, chans, cells)).reshape(tiles, chans, side, side)
        kernel = functools.partial(triangle_back_kernel, m == 1, tiles, kmax, chans)
        glr = tile_call(
            kernel, f"triangle_back{m}", lists(m), (lr, gprod), lr.shape, [pltpu.VMEM(lr.shape, F32)]
        )
        return exchange(glr.reshape(tiles, 2 * chans, cells)).reshape(wide, cells)

    def whole(*arrays):
        return [("w", array) for array in arrays]

    low_cells = (col, (channels, cells), BF16)
    lr_cells = (col, (wide, cells), BF16)
    square = ("w", (channels, channels), F32)
    broad = ("w", (channels, 2 * wide), F32)
    rows_out = (row, (cells, channels), BF16)

    (lr0,) = cellwise(first_kernel, "first", [(row, x)] + whole(*weights[0]), [lr_cells], cells)
    lr0, prod0 = triangle(lr0, 0)
    pair1, lr1 = cellwise(
        middle_kernel, "middle",
        [(row, x), (col, prod0)] + whole(w_gate[0], w_out[0], *weights[1]),
        [low_cells, lr_cells], cells,
    )
    lr1, prod1 = triangle(lr1, 1)
    new_pair, gprod1, glogit1, dgate1, dout1 = cellwise(
        top_kernel, "top",
        [(col, pair1), (col, prod1), (row, cot)] + whole(w_gate[1], w_out[1]),
        [rows_out, low_cells, low_cells, square, square], cells,
    )
    glr1 = triangle_back(lr1, gprod1, 1)
    upstream, gprod0, glogit0, dpair1, dgate0, dout0 = cellwise(
        turn_kernel, "turn",
        [(row if a is cot or a is x else col, a) for a in (pair1, cot, glr1, glogit1, x, prod0)]
        + whole(*weights[1], w_gate[1], w_gate[0], w_out[0]),
        [(col, (channels, cells), F32), low_cells, low_cells, broad, square, square], cells,
    )
    glr0 = triangle_back(lr0, gprod0, 0)
    d_pair, dpair0 = cellwise(
        last_kernel, "last",
        [(row, x), (col, upstream), (col, glr0), (col, glogit0)] + whole(*weights[0], w_gate[0]),
        [rows_out, broad], cells,
    )

    scale = 1.0 / math.sqrt(tiles * side * side)

    def scatter(*grads):
        joined = jnp.concatenate(grads, axis=1)
        return lax.psum_scatter(joined, "tile", scatter_dimension=0, tiled=True) * scale

    def unpermute(pair):
        pair = pair.reshape(-1, 2, devices, 2, chans).transpose(0, 3, 1, 2, 4)
        return pair.reshape(-1, 2 * wide)

    early = scatter(dpair1, dgate1, dout1, dgate0, dout0)
    late = scatter(dpair0)
    ends = [2 * wide + channels * n for n in range(5)]
    dgate1, dout1, dgate0, dout0 = [early[:, a:b] for a, b in zip(ends, ends[1:])]
    return (
        new_pair.reshape(pair_tiles.shape),
        d_pair.reshape(pair_tiles.shape),
        jnp.stack([unpermute(late), unpermute(early[:, : 2 * wide])]),
        jnp.stack([dgate0, dgate1]),
        jnp.stack([dout0, dout1]),
    )


def solution(mesh):
    cells = P(("groups", "tile"), None, None, None)
    in_specs = (cells, cells, P(), P(), P(), P(None, "groups", None, None), P(None, "groups"))
    grads = P("groups", "tile", None)
    return jax.shard_map(
        functools.partial(local, mesh.shape["tile"]), mesh=mesh, in_specs=in_specs,
        out_specs=(cells, cells, grads, grads, grads), check_vma=False,
    )
```

```python
import functools
import math

import jax
import jax.numpy as jnp
from jax import lax
from jax.experimental import pallas as pl
from jax.experimental.pallas import tpu as pltpu
from jax.sharding import PartitionSpec as P

EPS = 1e-05
CHUNK = 512
VMEM_BYTES = 40 * 1024 * 1024
F32, BF16 = jnp.float32, jnp.bfloat16


def dot(one, other, one_dim, other_dim):
    return lax.dot_general(one, other, (((one_dim,), (other_dim,)), ((), ())), preferred_element_type=F32)


def sigmoid(values):
    return 0.5 * jnp.tanh(0.5 * values) + 0.5


def normalize(values):
    shifted = values - jnp.mean(values, axis=0, keepdims=True)
    factor = lax.rsqrt(jnp.mean(shifted * shifted, axis=0, keepdims=True) + EPS)
    return shifted * factor, factor


def norm_back(upstream, normed, factor):
    first_mean = jnp.mean(upstream, axis=0, keepdims=True)
    cross_mean = jnp.mean(upstream * normed, axis=0, keepdims=True)
    return factor * (upstream - first_mean - normed * cross_mean)


def gated(normed_low, w_val, w_sig):
    return dot(w_val, normed_low, 1, 0), sigmoid(dot(w_sig, normed_low, 1, 0))


def project_in(pair, w_val, w_sig, lr_ref):
    normed_low = normalize(pair)[0].astype(BF16)
    value, sig = gated(normed_low, w_val[...], w_sig[...])
    lr_ref[...] = (value * sig).astype(BF16)


def out_parts(pair, prod_ref, w_gate, w_out):
    in_low = normalize(pair)[0].astype(BF16)
    gate = sigmoid(dot(w_gate[...], in_low, 0, 0))
    normed, factor = normalize(prod_ref[...].astype(F32))
    normed_low = normed.astype(BF16)
    update = dot(w_out[...], normed_low, 0, 0)
    return in_low, gate, normed, factor, normed_low, update


def accumulate(ref, value):
    @pl.when(pl.program_id(0) == 0)
    def _():
        ref[...] = jnp.zeros_like(ref)

    ref[...] += value


def back_out(upstream, parts, w_out, gprod_ref, glogit_ref, dgate_ref, dout_ref):
    in_low, gate, normed, factor, normed_low, update = parts
    grad_update = (upstream * gate).astype(BF16)
    grad_logit = (upstream * update * gate * (1.0 - gate)).astype(BF16)
    glogit_ref[...] = grad_logit
    accumulate(dout_ref, dot(normed_low, grad_update, 1, 1))
    accumulate(dgate_ref, dot(in_low, grad_logit, 1, 1))
    grad_normed = dot(w_out[...], grad_update, 1, 0)
    gprod_ref[...] = norm_back(grad_normed, normed, factor).astype(BF16)


def back_in(upstream, pair, glr_ref, glogit_ref, w_val, w_sig, w_gate, dpair_ref):
    normed, factor = normalize(pair)
    normed_low = normed.astype(BF16)
    value, sig = gated(normed_low, w_val[...], w_sig[...])
    flow = glr_ref[...].astype(F32)
    grad_val = flow * sig
    grad_sig = (grad_val * value * (1.0 - sig)).astype(BF16)
    grad_val = grad_val.astype(BF16)
    rows = grad_val.shape[0]
    accumulate(dpair_ref.at[:, :rows], dot(normed_low, grad_val, 1, 1))
    accumulate(dpair_ref.at[:, rows:], dot(normed_low, grad_sig, 1, 1))
    grad_normed = (
        dot(w_val[...], grad_val, 0, 0)
        + dot(w_sig[...], grad_sig, 0, 0)
        + dot(w_gate[...], glogit_ref[...], 1, 0)
    )
    return upstream + norm_back(grad_normed, normed, factor)


def turned(ref):
    return ref[...].astype(F32).T


def first_kernel(x_ref, wv, ws, lr_ref):
    project_in(turned(x_ref), wv, ws, lr_ref)


def middle_kernel(x_ref, prod_ref, wgate, wout, wv, ws, pair_ref, lr_ref):
    pair = turned(x_ref)
    _, gate, _, _, _, update = out_parts(pair, prod_ref, wgate, wout)
    low = (pair + gate * update).astype(BF16)
    pair_ref[...] = low
    project_in(low.astype(F32), wv, ws, lr_ref)


def top_kernel(pair_ref, prod_ref, cot_ref, wgate, wout, new_ref, gprod_ref, glogit_ref, dgate_ref, dout_ref):
    pair = pair_ref[...].astype(F32)
    parts = out_parts(pair, prod_ref, wgate, wout)
    new_ref[...] = (pair + parts[1] * parts[5]).T.astype(BF16)
    back_out(turned(cot_ref), parts, wout, gprod_ref, glogit_ref, dgate_ref, dout_ref)


def turn_kernel(
    pair_ref, cot_ref, glr_ref, glogit1_ref, x_ref, prod_ref, wv1, ws1, wgate1, wgate0, wout0,
    up_ref, gprod_ref, glogit_ref, dpair_ref, dgate_ref, dout_ref,
):
    upstream = back_in(
        turned(cot_ref), pair_ref[...].astype(F32), glr_ref, glogit1_ref, wv1, ws1, wgate1, dpair_ref
    )
    up_ref[...] = upstream
    parts = out_parts(turned(x_ref), prod_ref, wgate0, wout0)
    back_out(upstream, parts, wout0, gprod_ref, glogit_ref, dgate_ref, dout_ref)


def last_kernel(x_ref, up_ref, glr_ref, glogit_ref, wv, ws, wgate, dx_ref, dpair_ref):
    grad = back_in(up_ref[...], turned(x_ref), glr_ref, glogit_ref, wv, ws, wgate, dpair_ref)
    dx_ref[...] = grad.T.astype(BF16)


def cellwise(kernel, name, args, outs, cells):
    step = min(CHUNK, cells)

    def spec(kind, shape):
        if kind == "r":
            return pl.BlockSpec((step, shape[1]), lambda n: (n, 0))
        if kind == "c":
            return pl.BlockSpec((shape[0], step), lambda n: (0, n))
        return pl.BlockSpec(shape, lambda n: (0, 0))

    return pl.pallas_call(
        kernel,
        name=name,
        grid=(cells // step,),
        in_specs=[spec(kind, array.shape) for kind, array in args],
        out_specs=[spec(kind, shape) for kind, shape, _ in outs],
        out_shape=[jax.ShapeDtypeStruct(shape, kind) for _, shape, kind in outs],
        compiler_params=pltpu.CompilerParams(vmem_limit_bytes=VMEM_BYTES),
    )(*[array for _, array in args])


def triangle_kernel(incoming, tiles, kmax, chans, lists, counts, lr_ref, prod_ref):
    dim = 0 if incoming else 1

    def one(tile, _):
        def term(slot, chan):
            base = (tile * kmax + slot) * 2
            return dot(lr_ref[lists[base], chan], lr_ref[lists[base + 1], chans + chan], dim, dim)

        used = counts[tile]
        for chan in range(chans):
            total = term(0, chan)
            for slot in range(1, kmax):
                total = total + jnp.where(slot < used, term(slot, chan), 0.0)
            prod_ref[tile, chan] = total.astype(BF16)
        return 0

    lax.fori_loop(0, tiles, one, 0)


def triangle_back_kernel(incoming, tiles, kmax, chans, lists, counts, lr_ref, gprod_ref, glr_ref, total):
    total[...] = jnp.zeros_like(total)

    def one(tile, _):
        for slot in range(kmax):

            @pl.when(slot < counts[tile])
            def _():
                base = (tile * kmax + slot) * 2
                x, y = lists[base], lists[base + 1]
                for chan in range(chans):
                    grad = gprod_ref[tile, chan]
                    left, right = lr_ref[x, chan], lr_ref[y, chans + chan]
                    if incoming:
                        total[x, chan] += dot(right, grad, 1, 1)
                        total[y, chans + chan] += dot(left, grad, 1, 0)
                    else:
                        total[x, chan] += dot(grad, right, 1, 0)
                        total[y, chans + chan] += dot(grad, left, 0, 0)
        return 0

    lax.fori_loop(0, tiles, one, 0)

    def store(tile, _):
        glr_ref[tile] = total[tile].astype(BF16)
        return 0

    lax.fori_loop(0, tiles, store, 0)


def tile_call(kernel, name, scalars, arrays, out_shape, scratch):
    return pl.pallas_call(
        kernel,
        name=name,
        in_specs=[pl.BlockSpec(memory_space=pltpu.SMEM)] * len(scalars)
        + [pl.BlockSpec(memory_space=pltpu.VMEM)] * len(arrays),
        out_specs=pl.BlockSpec(memory_space=pltpu.VMEM),
        out_shape=jax.ShapeDtypeStruct(out_shape, BF16),
        scratch_shapes=scratch,
        compiler_params=pltpu.CompilerParams(vmem_limit_bytes=VMEM_BYTES),
    )(*scalars, *arrays)


def exchange_kernel(amount, devices, *refs):
    sources, targets = refs[:amount], refs[amount : 2 * amount]
    send_sem, recv_sem, own_sem = refs[2 * amount :]
    me = lax.axis_index("tile")
    barrier = pltpu.get_barrier_semaphore()

    def greet(offset, _):
        peer = lax.rem(me + offset, devices)
        pl.semaphore_signal(
            barrier, inc=1, device_id={"tile": peer}, device_id_type=pl.DeviceIdType.MESH
        )
        return 0

    lax.fori_loop(1, devices, greet, 0)
    own = [
        pltpu.make_async_copy(source.at[me], target.at[me], own_sem.at[n])
        for n, (source, target) in enumerate(zip(sources, targets))
    ]
    for copy in own:
        copy.start()
    pl.semaphore_wait(barrier, devices - 1)

    def copies(offset):
        peer = lax.rem(me + offset, devices)
        return [
            pltpu.make_async_remote_copy(
                src_ref=source.at[peer],
                dst_ref=target.at[me],
                send_sem=send_sem.at[n, offset],
                recv_sem=recv_sem.at[n, offset],
                device_id={"tile": peer},
                device_id_type=pl.DeviceIdType.MESH,
            )
            for n, (source, target) in enumerate(zip(sources, targets))
        ]

    def begin(place, _):
        far = (place + 1) // 2
        for copy in copies(devices // 2 + far * (1 - 2 * lax.rem(place, 2))):
            copy.start()
        return 0

    def finish(offset, _):
        for copy in copies(offset):
            copy.wait()
        return 0

    lax.fori_loop(0, devices - 1, begin, 0)
    lax.fori_loop(1, devices, finish, 0)
    for copy in own:
        copy.wait()


def exchange(number, *arrays):
    amount, devices = len(arrays), arrays[0].shape[0]
    return pl.pallas_call(
        functools.partial(exchange_kernel, amount, devices),
        name=f"exchange{number}",
        in_specs=[pl.BlockSpec(memory_space=pl.ANY)] * amount,
        out_specs=[pl.BlockSpec(memory_space=pl.ANY)] * amount,
        out_shape=[jax.ShapeDtypeStruct(a.shape, a.dtype) for a in arrays],
        scratch_shapes=[
            pltpu.SemaphoreType.DMA((amount, devices)),
            pltpu.SemaphoreType.DMA((amount, devices)),
            pltpu.SemaphoreType.DMA((amount,)),
        ],
        compiler_params=pltpu.CompilerParams(collective_id=number, has_side_effects=True),
    )(*arrays)


def local(devices, pair_tiles, cotangent, w_pair, w_gate, w_out, tile_lists, list_counts):
    owned, side, _, channels = pair_tiles.shape
    cells = owned * side * side
    tiles, kmax = tile_lists.shape[1], tile_lists.shape[2]
    chans = channels // devices
    x = pair_tiles.reshape(cells, channels)
    cot = cotangent.reshape(cells, channels)
    weights = w_pair.reshape(2, channels, 2, 2, devices, chans)
    weights = weights.transpose(0, 3, 4, 2, 5, 1).reshape(2, 2, 2 * channels, channels)
    wide = 2 * channels
    col, row = "c", "r"

    def lists(m):
        return tile_lists[m].reshape(-1), list_counts[m]

    def triangle(lr, m):
        (lr,) = exchange(2 * m, lr.reshape(devices, 2 * chans, cells))
        lr = lr.reshape(tiles, 2 * chans, side, side)
        kernel = functools.partial(triangle_kernel, m == 1, tiles, kmax, chans)
        prod = tile_call(kernel, f"triangle{m}", lists(m), (lr,), (tiles, chans, side, side), [])
        (prod,) = exchange(2 * m + 1, prod.reshape(tiles, chans, cells))
        return lr, prod.reshape(channels, cells)

    def triangle_back(lr, gprod, m, *others):
        (gprod,) = exchange(4 + 2 * m, gprod.reshape(devices, chans, cells))
        gprod = gprod.reshape(tiles, chans, side, side)
        kernel = functools.partial(triangle_back_kernel, m == 1, tiles, kmax, chans)
        glr = tile_call(
            kernel, f"triangle_back{m}", lists(m), (lr, gprod), lr.shape, [pltpu.VMEM(lr.shape, F32)]
        )
        glr, *others = exchange(5 + 2 * m, glr.reshape(tiles, 2 * chans, cells), *others)
        return glr.reshape(wide, cells), *others

    def by_rows(grad):
        return grad.reshape(devices, channels // devices, -1)

    def whole(*arrays):
        return [("w", array) for array in arrays]

    low_cells = (col, (channels, cells), BF16)
    lr_cells = (col, (wide, cells), BF16)
    square = ("w", (channels, channels), F32)
    broad = ("w", (channels, 2 * wide), F32)
    rows_out = (row, (cells, channels), BF16)

    (lr0,) = cellwise(first_kernel, "first", [(row, x)] + whole(*weights[0]), [lr_cells], cells)
    lr0, prod0 = triangle(lr0, 0)
    pair1, lr1 = cellwise(
        middle_kernel, "middle",
        [(row, x), (col, prod0)] + whole(w_gate[0], w_out[0], *weights[1]),
        [low_cells, lr_cells], cells,
    )
    lr1, prod1 = triangle(lr1, 1)
    new_pair, gprod1, glogit1, dgate1, dout1 = cellwise(
        top_kernel, "top",
        [(col, pair1), (col, prod1), (row, cot)] + whole(w_gate[1], w_out[1]),
        [rows_out, low_cells, low_cells, square, square], cells,
    )
    (glr1,) = triangle_back(lr1, gprod1, 1)
    upstream, gprod0, glogit0, dpair1, dgate0, dout0 = cellwise(
        turn_kernel, "turn",
        [(row if a is cot or a is x else col, a) for a in (pair1, cot, glr1, glogit1, x, prod0)]
        + whole(*weights[1], w_gate[1], w_gate[0], w_out[0]),
        [(col, (channels, cells), F32), low_cells, low_cells, broad, square, square], cells,
    )
    early = jnp.concatenate([dpair1, dgate1, dout1, dgate0, dout0], axis=1)
    glr0, early = triangle_back(lr0, gprod0, 0, by_rows(early))
    d_pair, dpair0 = cellwise(
        last_kernel, "last",
        [(row, x), (col, upstream), (col, glr0), (col, glogit0)] + whole(*weights[0], w_gate[0]),
        [rows_out, broad], cells,
    )

    scale = 1.0 / math.sqrt(tiles * side * side)

    def unpermute(pair):
        pair = pair.reshape(-1, 2, devices, 2, chans).transpose(0, 3, 1, 2, 4)
        return pair.reshape(-1, 2 * wide)

    early = jnp.sum(early, axis=0) * scale
    late = jnp.sum(exchange(8, by_rows(dpair0))[0], axis=0) * scale
    ends = [2 * wide + channels * n for n in range(5)]
    dgate1, dout1, dgate0, dout0 = [early[:, a:b] for a, b in zip(ends, ends[1:])]
    return (
        new_pair.reshape(pair_tiles.shape),
        d_pair.reshape(pair_tiles.shape),
        jnp.stack([unpermute(late), unpermute(early[:, : 2 * wide])]),
        jnp.stack([dgate0, dgate1]),
        jnp.stack([dout0, dout1]),
    )


def solution(mesh):
    cells = P(("groups", "tile"), None, None, None)
    in_specs = (cells, cells, P(), P(), P(), P(None, "groups", None, None), P(None, "groups"))
    grads = P("groups", "tile", None)
    return jax.shard_map(
        functools.partial(local, mesh.shape["tile"]), mesh=mesh, in_specs=in_specs,
        out_specs=(cells, cells, grads, grads, grads), check_vma=False,
    )
```

```python
import functools
import math

import jax
import jax.numpy as jnp
from jax import lax
from jax.experimental import pallas as pl
from jax.experimental.pallas import tpu as pltpu
from jax.sharding import PartitionSpec as P

EPS = 1e-05
CHUNK = 512
VMEM_BYTES = 40 * 1024 * 1024
F32, BF16 = jnp.float32, jnp.bfloat16


def dot(one, other, one_dim, other_dim):
    return lax.dot_general(one, other, (((one_dim,), (other_dim,)), ((), ())), preferred_element_type=F32)


def sigmoid(values):
    return 0.5 * jnp.tanh(0.5 * values) + 0.5


def normalize(values):
    shifted = values - jnp.mean(values, axis=0, keepdims=True)
    factor = lax.rsqrt(jnp.mean(shifted * shifted, axis=0, keepdims=True) + EPS)
    return shifted * factor, factor


def norm_back(upstream, normed, factor):
    first_mean = jnp.mean(upstream, axis=0, keepdims=True)
    cross_mean = jnp.mean(upstream * normed, axis=0, keepdims=True)
    return factor * (upstream - first_mean - normed * cross_mean)


def gated(normed_low, w_val, w_sig):
    return dot(w_val, normed_low, 1, 0), sigmoid(dot(w_sig, normed_low, 1, 0))


def project_in(pair, w_val, w_sig, lr_ref):
    normed_low = normalize(pair)[0].astype(BF16)
    value, sig = gated(normed_low, w_val[...], w_sig[...])
    lr_ref[...] = (value * sig).astype(BF16)


def out_parts(pair, prod_ref, w_gate, w_out):
    in_low = normalize(pair)[0].astype(BF16)
    gate = sigmoid(dot(w_gate[...], in_low, 0, 0))
    normed, factor = normalize(prod_ref[...].astype(F32))
    normed_low = normed.astype(BF16)
    update = dot(w_out[...], normed_low, 0, 0)
    return in_low, gate, normed, factor, normed_low, update


def accumulate(ref, value):
    @pl.when(pl.program_id(0) == 0)
    def _():
        ref[...] = jnp.zeros_like(ref)

    ref[...] += value


def back_out(upstream, parts, w_out, gprod_ref, glogit_ref, dgate_ref, dout_ref):
    in_low, gate, normed, factor, normed_low, update = parts
    grad_update = (upstream * gate).astype(BF16)
    grad_logit = (upstream * update * gate * (1.0 - gate)).astype(BF16)
    glogit_ref[...] = grad_logit
    accumulate(dout_ref, dot(normed_low, grad_update, 1, 1))
    accumulate(dgate_ref, dot(in_low, grad_logit, 1, 1))
    grad_normed = dot(w_out[...], grad_update, 1, 0)
    gprod_ref[...] = norm_back(grad_normed, normed, factor).astype(BF16)


def back_in(upstream, pair, glr_ref, glogit_ref, w_val, w_sig, w_gate, dpair_ref):
    normed, factor = normalize(pair)
    normed_low = normed.astype(BF16)
    value, sig = gated(normed_low, w_val[...], w_sig[...])
    flow = glr_ref[...].astype(F32)
    grad_val = flow * sig
    grad_sig = (grad_val * value * (1.0 - sig)).astype(BF16)
    grad_val = grad_val.astype(BF16)
    rows = grad_val.shape[0]
    accumulate(dpair_ref.at[:, :rows], dot(normed_low, grad_val, 1, 1))
    accumulate(dpair_ref.at[:, rows:], dot(normed_low, grad_sig, 1, 1))
    grad_normed = (
        dot(w_val[...], grad_val, 0, 0)
        + dot(w_sig[...], grad_sig, 0, 0)
        + dot(w_gate[...], glogit_ref[...], 1, 0)
    )
    return upstream + norm_back(grad_normed, normed, factor)


def turned(ref):
    values = jnp.swapaxes(ref[...], 0, 1).astype(F32)
    return values.reshape(-1, values.shape[-1]).T


def turn_back(ref, values):
    _, rows, side, channels = ref.shape
    ref[...] = jnp.swapaxes(values.T.reshape(rows, 2, side, channels), 0, 1).astype(ref.dtype)


def first_kernel(x_ref, wv, ws, lr_ref):
    project_in(turned(x_ref), wv, ws, lr_ref)


def middle_kernel(x_ref, prod_ref, wgate, wout, wv, ws, pair_ref, lr_ref):
    pair = turned(x_ref)
    _, gate, _, _, _, update = out_parts(pair, prod_ref, wgate, wout)
    low = (pair + gate * update).astype(BF16)
    pair_ref[...] = low
    project_in(low.astype(F32), wv, ws, lr_ref)


def top_kernel(pair_ref, prod_ref, cot_ref, wgate, wout, new_ref, gprod_ref, glogit_ref, dgate_ref, dout_ref):
    pair = pair_ref[...].astype(F32)
    parts = out_parts(pair, prod_ref, wgate, wout)
    turn_back(new_ref, pair + parts[1] * parts[5])
    back_out(turned(cot_ref), parts, wout, gprod_ref, glogit_ref, dgate_ref, dout_ref)


def turn_kernel(
    pair_ref, cot_ref, glr_ref, glogit1_ref, x_ref, prod_ref, wv1, ws1, wgate1, wgate0, wout0,
    up_ref, gprod_ref, glogit_ref, dpair_ref, dgate_ref, dout_ref,
):
    upstream = back_in(
        turned(cot_ref), pair_ref[...].astype(F32), glr_ref, glogit1_ref, wv1, ws1, wgate1, dpair_ref
    )
    up_ref[...] = upstream
    parts = out_parts(turned(x_ref), prod_ref, wgate0, wout0)
    back_out(upstream, parts, wout0, gprod_ref, glogit_ref, dgate_ref, dout_ref)


def last_kernel(x_ref, up_ref, glr_ref, glogit_ref, wv, ws, wgate, dx_ref, dpair_ref):
    grad = back_in(up_ref[...], turned(x_ref), glr_ref, glogit_ref, wv, ws, wgate, dpair_ref)
    turn_back(dx_ref, grad)


def cellwise(kernel, name, args, outs, cells):
    step = min(CHUNK, cells)

    def spec(kind, shape):
        if kind == "r":
            _, _, side, channels = shape
            return pl.BlockSpec((2, step // (2 * side), side, channels), lambda n: (0, n, 0, 0))
        if kind == "c":
            return pl.BlockSpec((shape[0], step), lambda n: (0, n))
        return pl.BlockSpec(shape, lambda n: (0, 0))

    return pl.pallas_call(
        kernel,
        name=name,
        grid=(cells // step,),
        in_specs=[spec(kind, array.shape) for kind, array in args],
        out_specs=[spec(kind, shape) for kind, shape, _ in outs],
        out_shape=[jax.ShapeDtypeStruct(shape, kind) for _, shape, kind in outs],
        compiler_params=pltpu.CompilerParams(vmem_limit_bytes=VMEM_BYTES),
    )(*[array for _, array in args])


def unfold(folded):
    side = folded.shape[1] // 2
    return jnp.concatenate([folded[:, :side], folded[:, side:]], axis=0)


def fold(square):
    half = square.shape[0] // 2
    return jnp.concatenate([square[:half], square[half:]], axis=1)


def triangle_kernel(incoming, tiles, kmax, lists, counts, lr_ref, prod_ref):
    dim = 0 if incoming else 1

    def one(tile, _):
        def term(slot):
            base = (tile * kmax + slot) * 2
            left = unfold(lr_ref[lists[base], 0, 0])
            return dot(left, unfold(lr_ref[lists[base + 1], 1, 0]), dim, dim)

        total = term(0)
        for slot in range(1, kmax):
            total = total + jnp.where(slot < counts[tile], term(slot), 0.0)
        prod_ref[tile, 0] = fold(total).astype(BF16)
        return 0

    lax.fori_loop(0, tiles, one, 0, unroll=8)


def triangle_back_kernel(incoming, tiles, kmax, lists, counts, lr_ref, gprod_ref, glr_ref, total):
    total[...] = jnp.zeros_like(total)

    def one(tile, _):
        grad = unfold(gprod_ref[tile, 0])
        for slot in range(kmax):

            def add():
                base = (tile * kmax + slot) * 2
                x, y = lists[base], lists[base + 1]
                left, right = unfold(lr_ref[x, 0, 0]), unfold(lr_ref[y, 1, 0])
                if incoming:
                    total[0, x] += dot(right, grad, 1, 1)
                    total[1, y] += dot(left, grad, 1, 0)
                else:
                    total[0, x] += dot(grad, right, 1, 0)
                    total[1, y] += dot(grad, left, 0, 0)

            if slot == 0:
                add()
            else:
                pl.when(slot < counts[tile])(add)
        return 0

    lax.fori_loop(0, tiles, one, 0, unroll=4)

    def store(tile, _):
        for which in range(2):
            glr_ref[tile, which, 0] = fold(total[which, tile]).astype(BF16)
        return 0

    lax.fori_loop(0, tiles, store, 0, unroll=4)


def tile_call(kernel, name, scalars, arrays, out_shape, scratch):
    def spec(shape):
        lead = len(shape) - 3
        return pl.BlockSpec(shape[:lead] + (1,) + shape[-2:], lambda n: (0,) * lead + (n, 0, 0))

    return pl.pallas_call(
        kernel,
        name=name,
        grid=(out_shape[-3],),
        in_specs=[pl.BlockSpec(memory_space=pltpu.SMEM)] * len(scalars)
        + [spec(array.shape) for array in arrays],
        out_specs=spec(out_shape),
        out_shape=jax.ShapeDtypeStruct(out_shape, BF16),
        scratch_shapes=scratch,
        compiler_params=pltpu.CompilerParams(vmem_limit_bytes=VMEM_BYTES),
    )(*scalars, *arrays)


def exchange_kernel(amount, devices, *refs):
    sources, targets = refs[:amount], refs[amount : 2 * amount]
    send_sem, recv_sem, own_sem = refs[2 * amount :]
    me = lax.axis_index("tile")
    barrier = pltpu.get_barrier_semaphore()

    def greet(offset, _):
        peer = lax.rem(me + offset, devices)
        pl.semaphore_signal(
            barrier, inc=1, device_id={"tile": peer}, device_id_type=pl.DeviceIdType.MESH
        )
        return 0

    lax.fori_loop(1, devices, greet, 0)
    own = [
        pltpu.make_async_copy(source.at[me], target.at[me], own_sem.at[n])
        for n, (source, target) in enumerate(zip(sources, targets))
    ]
    for copy in own:
        copy.start()
    pl.semaphore_wait(barrier, devices - 1)

    def copies(offset):
        peer = lax.rem(me + offset, devices)
        return [
            pltpu.make_async_remote_copy(
                src_ref=source.at[peer],
                dst_ref=target.at[me],
                send_sem=send_sem.at[n, offset],
                recv_sem=recv_sem.at[n, offset],
                device_id={"tile": peer},
                device_id_type=pl.DeviceIdType.MESH,
            )
            for n, (source, target) in enumerate(zip(sources, targets))
        ]

    def begin(place, _):
        far = (place + 1) // 2
        for copy in copies(devices // 2 + far * (1 - 2 * lax.rem(place, 2))):
            copy.start()
        return 0

    def finish(offset, _):
        for copy in copies(offset):
            copy.wait()
        return 0

    lax.fori_loop(0, devices - 1, begin, 0)
    lax.fori_loop(1, devices, finish, 0)
    for copy in own:
        copy.wait()


def exchange(number, *arrays):
    amount, devices = len(arrays), arrays[0].shape[0]
    return pl.pallas_call(
        functools.partial(exchange_kernel, amount, devices),
        name=f"exchange{number}",
        in_specs=[pl.BlockSpec(memory_space=pl.ANY)] * amount,
        out_specs=[pl.BlockSpec(memory_space=pl.ANY)] * amount,
        out_shape=[jax.ShapeDtypeStruct(a.shape, a.dtype) for a in arrays],
        scratch_shapes=[
            pltpu.SemaphoreType.DMA((amount, devices)),
            pltpu.SemaphoreType.DMA((amount, devices)),
            pltpu.SemaphoreType.DMA((amount,)),
        ],
        compiler_params=pltpu.CompilerParams(collective_id=number, has_side_effects=True),
    )(*arrays)


def local(devices, pair_tiles, cotangent, w_pair, w_gate, w_out, tile_lists, list_counts):
    owned, side, _, channels = pair_tiles.shape
    cells = owned * side * side
    tiles, kmax = tile_lists.shape[1], tile_lists.shape[2]
    chans = channels // devices
    x = pair_tiles.reshape(2, side // 2, side, channels)
    cot = cotangent.reshape(x.shape)
    weights = w_pair.reshape(2, channels, 2, 2, devices, chans)
    weights = weights.transpose(0, 3, 4, 2, 5, 1).reshape(2, 2, 2 * channels, channels)
    wide = 2 * channels
    col, row = "c", "r"

    def lists(m):
        return tile_lists[m].reshape(-1), list_counts[m]

    folded = (side // 2, 2 * side)

    def triangle(lr, m):
        (lr,) = exchange(2 * m, lr.reshape(devices, 2 * chans, cells))
        lr = lr.reshape(tiles, 2, chans, *folded)
        kernel = functools.partial(triangle_kernel, m == 1, tiles, kmax)
        prod = tile_call(kernel, f"triangle{m}", lists(m), (lr,), (tiles, chans, *folded), [])
        (prod,) = exchange(2 * m + 1, prod.reshape(tiles, chans, cells))
        return lr, prod.reshape(channels, cells)

    def triangle_back(lr, gprod, m, *others):
        (gprod,) = exchange(4 + 2 * m, gprod.reshape(devices, chans, cells))
        gprod = gprod.reshape(tiles, chans, *folded)
        kernel = functools.partial(triangle_back_kernel, m == 1, tiles, kmax)
        sums = pltpu.VMEM((2, tiles, side, side), F32)
        glr = tile_call(kernel, f"triangle_back{m}", lists(m), (lr, gprod), lr.shape, [sums])
        glr, *others = exchange(5 + 2 * m, glr.reshape(tiles, 2 * chans, cells), *others)
        return glr.reshape(wide, cells), *others

    def by_rows(grad):
        return grad.astype(BF16).reshape(devices, channels // devices, -1)

    def whole(*arrays):
        return [("w", array) for array in arrays]

    low_cells = (col, (channels, cells), BF16)
    lr_cells = (col, (wide, cells), BF16)
    square = ("w", (channels, channels), F32)
    broad = ("w", (channels, 2 * wide), F32)
    rows_out = (row, x.shape, BF16)

    (lr0,) = cellwise(first_kernel, "first", [(row, x)] + whole(*weights[0]), [lr_cells], cells)
    lr0, prod0 = triangle(lr0, 0)
    pair1, lr1 = cellwise(
        middle_kernel, "middle",
        [(row, x), (col, prod0)] + whole(w_gate[0], w_out[0], *weights[1]),
        [low_cells, lr_cells], cells,
    )
    lr1, prod1 = triangle(lr1, 1)
    new_pair, gprod1, glogit1, dgate1, dout1 = cellwise(
        top_kernel, "top",
        [(col, pair1), (col, prod1), (row, cot)] + whole(w_gate[1], w_out[1]),
        [rows_out, low_cells, low_cells, square, square], cells,
    )
    (glr1,) = triangle_back(lr1, gprod1, 1)
    upstream, gprod0, glogit0, dpair1, dgate0, dout0 = cellwise(
        turn_kernel, "turn",
        [(row if a is cot or a is x else col, a) for a in (pair1, cot, glr1, glogit1, x, prod0)]
        + whole(*weights[1], w_gate[1], w_gate[0], w_out[0]),
        [(col, (channels, cells), F32), low_cells, low_cells, broad, square, square], cells,
    )
    early = jnp.concatenate([dpair1, dgate1, dout1, dgate0, dout0], axis=1)
    glr0, early = triangle_back(lr0, gprod0, 0, by_rows(early))
    d_pair, dpair0 = cellwise(
        last_kernel, "last",
        [(row, x), (col, upstream), (col, glr0), (col, glogit0)] + whole(*weights[0], w_gate[0]),
        [rows_out, broad], cells,
    )

    scale = 1.0 / math.sqrt(tiles * side * side)

    def unpermute(pair):
        pair = pair.reshape(-1, 2, devices, 2, chans).transpose(0, 3, 1, 2, 4)
        return pair.reshape(-1, 2 * wide)

    early = jnp.sum(early.astype(F32), axis=0) * scale
    late = jnp.sum(exchange(8, by_rows(dpair0))[0].astype(F32), axis=0) * scale
    ends = [2 * wide + channels * n for n in range(5)]
    dgate1, dout1, dgate0, dout0 = [early[:, a:b] for a, b in zip(ends, ends[1:])]
    return (
        new_pair.reshape(pair_tiles.shape),
        d_pair.reshape(pair_tiles.shape),
        jnp.stack([unpermute(late), unpermute(early[:, : 2 * wide])]),
        jnp.stack([dgate0, dgate1]),
        jnp.stack([dout0, dout1]),
    )


def solution(mesh):
    cells = P(("groups", "tile"), None, None, None)
    in_specs = (cells, cells, P(), P(), P(), P(None, "groups", None, None), P(None, "groups"))
    grads = P("groups", "tile", None)
    return jax.shard_map(
        functools.partial(local, mesh.shape["tile"]), mesh=mesh, in_specs=in_specs,
        out_specs=(cells, cells, grads, grads, grads), check_vma=False,
    )
```

```python
import functools
import math

import jax
import jax.numpy as jnp
from jax import lax
from jax.experimental import pallas as pl
from jax.experimental.pallas import tpu as pltpu
from jax.sharding import PartitionSpec as P

EPS = 1e-05
CHUNK = 512
VMEM_BYTES = 40 * 1024 * 1024
F32, BF16 = jnp.float32, jnp.bfloat16


def dot(one, other, one_dim, other_dim):
    return lax.dot_general(one, other, (((one_dim,), (other_dim,)), ((), ())), preferred_element_type=F32)


def sigmoid(values):
    return 0.5 * jnp.tanh(0.5 * values) + 0.5


def normalize(values):
    shifted = values - jnp.mean(values, axis=0, keepdims=True)
    factor = lax.rsqrt(jnp.mean(shifted * shifted, axis=0, keepdims=True) + EPS)
    return shifted * factor, factor


def norm_back(upstream, normed, factor):
    first_mean = jnp.mean(upstream, axis=0, keepdims=True)
    cross_mean = jnp.mean(upstream * normed, axis=0, keepdims=True)
    return factor * (upstream - first_mean - normed * cross_mean)


def gated(normed_low, w_val, w_sig):
    return dot(w_val, normed_low, 1, 0), sigmoid(dot(w_sig, normed_low, 1, 0))


def project_in(pair, w_val, w_sig, lr_ref):
    normed_low = normalize(pair)[0].astype(BF16)
    value, sig = gated(normed_low, w_val[...], w_sig[...])
    lr_ref[...] = (value * sig).astype(BF16)


def out_parts(pair, prod_ref, w_gate, w_out):
    in_low = normalize(pair)[0].astype(BF16)
    gate = sigmoid(dot(w_gate[...], in_low, 0, 0))
    normed, factor = normalize(prod_ref[...].astype(F32))
    normed_low = normed.astype(BF16)
    update = dot(w_out[...], normed_low, 0, 0)
    return in_low, gate, normed, factor, normed_low, update


def accumulate(ref, value):
    @pl.when(pl.program_id(0) == 0)
    def _():
        ref[...] = jnp.zeros_like(ref)

    ref[...] += value


def back_out(upstream, parts, w_out, gprod_ref, glogit_ref, dgate_ref, dout_ref):
    in_low, gate, normed, factor, normed_low, update = parts
    grad_update = (upstream * gate).astype(BF16)
    grad_logit = (upstream * update * gate * (1.0 - gate)).astype(BF16)
    glogit_ref[...] = grad_logit
    accumulate(dout_ref, dot(normed_low, grad_update, 1, 1))
    accumulate(dgate_ref, dot(in_low, grad_logit, 1, 1))
    grad_normed = dot(w_out[...], grad_update, 1, 0)
    gprod_ref[...] = norm_back(grad_normed, normed, factor).astype(BF16)


def back_in(upstream, pair, glr_ref, glogit_ref, w_val, w_sig, w_gate, dpair_ref):
    normed, factor = normalize(pair)
    normed_low = normed.astype(BF16)
    value, sig = gated(normed_low, w_val[...], w_sig[...])
    flow = glr_ref[...].astype(F32)
    grad_val = flow * sig
    grad_sig = (grad_val * value * (1.0 - sig)).astype(BF16)
    grad_val = grad_val.astype(BF16)
    rows = grad_val.shape[0]
    accumulate(dpair_ref.at[:, :rows], dot(normed_low, grad_val, 1, 1))
    accumulate(dpair_ref.at[:, rows:], dot(normed_low, grad_sig, 1, 1))
    grad_normed = (
        dot(w_val[...], grad_val, 0, 0)
        + dot(w_sig[...], grad_sig, 0, 0)
        + dot(w_gate[...], glogit_ref[...], 1, 0)
    )
    return upstream + norm_back(grad_normed, normed, factor)


def turned(ref):
    values = jnp.swapaxes(ref[...], 0, 1).astype(F32)
    return values.reshape(-1, values.shape[-1]).T


def turn_back(ref, values):
    _, rows, side, channels = ref.shape
    ref[...] = jnp.swapaxes(values.T.reshape(rows, 2, side, channels), 0, 1).astype(ref.dtype)


def first_kernel(x_ref, wv, ws, lr_ref):
    project_in(turned(x_ref), wv, ws, lr_ref)


def middle_kernel(x_ref, prod_ref, wgate, wout, wv, ws, pair_ref, lr_ref):
    pair = turned(x_ref)
    _, gate, _, _, _, update = out_parts(pair, prod_ref, wgate, wout)
    low = (pair + gate * update).astype(BF16)
    pair_ref[...] = low
    project_in(low.astype(F32), wv, ws, lr_ref)


def top_kernel(pair_ref, prod_ref, cot_ref, wgate, wout, new_ref, gprod_ref, glogit_ref, dgate_ref, dout_ref):
    pair = pair_ref[...].astype(F32)
    parts = out_parts(pair, prod_ref, wgate, wout)
    turn_back(new_ref, pair + parts[1] * parts[5])
    back_out(turned(cot_ref), parts, wout, gprod_ref, glogit_ref, dgate_ref, dout_ref)


def turn_kernel(
    pair_ref, cot_ref, glr_ref, glogit1_ref, x_ref, prod_ref, wv1, ws1, wgate1, wgate0, wout0,
    up_ref, gprod_ref, glogit_ref, dpair_ref, dgate_ref, dout_ref,
):
    upstream = back_in(
        turned(cot_ref), pair_ref[...].astype(F32), glr_ref, glogit1_ref, wv1, ws1, wgate1, dpair_ref
    )
    up_ref[...] = upstream
    parts = out_parts(turned(x_ref), prod_ref, wgate0, wout0)
    back_out(upstream, parts, wout0, gprod_ref, glogit_ref, dgate_ref, dout_ref)


def last_kernel(x_ref, up_ref, glr_ref, glogit_ref, wv, ws, wgate, dx_ref, dpair_ref):
    grad = back_in(up_ref[...], turned(x_ref), glr_ref, glogit_ref, wv, ws, wgate, dpair_ref)
    turn_back(dx_ref, grad)


def cellwise(kernel, name, args, outs, cells):
    step = min(CHUNK, cells)

    def spec(kind, shape):
        if kind == "r":
            _, _, side, channels = shape
            return pl.BlockSpec((2, step // (2 * side), side, channels), lambda n: (0, n, 0, 0))
        if kind == "c":
            return pl.BlockSpec((shape[0], step), lambda n: (0, n))
        return pl.BlockSpec(shape, lambda n: (0, 0))

    return pl.pallas_call(
        kernel,
        name=name,
        grid=(cells // step,),
        in_specs=[spec(kind, array.shape) for kind, array in args],
        out_specs=[spec(kind, shape) for kind, shape, _ in outs],
        out_shape=[jax.ShapeDtypeStruct(shape, kind) for _, shape, kind in outs],
        compiler_params=pltpu.CompilerParams(vmem_limit_bytes=VMEM_BYTES),
    )(*[array for _, array in args])


def unfold(folded):
    side = folded.shape[1] // 2
    return jnp.concatenate([folded[:, :side], folded[:, side:]], axis=0)


def fold(square):
    half = square.shape[0] // 2
    return jnp.concatenate([square[:half], square[half:]], axis=1)


def triangle_kernel(incoming, tiles, kmax, chans, lists, counts, lr_ref, prod_ref):
    dim = 0 if incoming else 1

    def one(tile, _):
        def term(slot, chan):
            base = (tile * kmax + slot) * 2
            left = unfold(lr_ref[lists[base], 0, chan])
            return dot(left, unfold(lr_ref[lists[base + 1], 1, chan]), dim, dim)

        used = counts[tile]
        for chan in range(chans):
            total = term(0, chan)
            for slot in range(1, kmax):
                total = total + jnp.where(slot < used, term(slot, chan), 0.0)
            prod_ref[tile, chan] = fold(total).astype(BF16)
        return 0

    lax.fori_loop(0, tiles, one, 0)


def triangle_back_kernel(incoming, tiles, kmax, chans, lists, counts, lr_ref, gprod_ref, glr_ref, total):
    total[...] = jnp.zeros_like(total)

    def one(tile, _):
        for slot in range(kmax):

            def add():
                base = (tile * kmax + slot) * 2
                x, y = lists[base], lists[base + 1]
                for chan in range(chans):
                    grad = unfold(gprod_ref[tile, chan])
                    left, right = unfold(lr_ref[x, 0, chan]), unfold(lr_ref[y, 1, chan])
                    if incoming:
                        total[x, 0, chan] += dot(right, grad, 1, 1)
                        total[y, 1, chan] += dot(left, grad, 1, 0)
                    else:
                        total[x, 0, chan] += dot(grad, right, 1, 0)
                        total[y, 1, chan] += dot(grad, left, 0, 0)

            if slot == 0:
                add()
            else:
                pl.when(slot < counts[tile])(add)
        return 0

    lax.fori_loop(0, tiles, one, 0)

    def store(tile, _):
        for which in range(2):
            for chan in range(chans):
                glr_ref[tile, which, chan] = fold(total[tile, which, chan]).astype(BF16)
        return 0

    lax.fori_loop(0, tiles, store, 0)


def tile_call(kernel, name, scalars, arrays, out_shape, scratch):
    return pl.pallas_call(
        kernel,
        name=name,
        in_specs=[pl.BlockSpec(memory_space=pltpu.SMEM)] * len(scalars)
        + [pl.BlockSpec(memory_space=pltpu.VMEM)] * len(arrays),
        out_specs=pl.BlockSpec(memory_space=pltpu.VMEM),
        out_shape=jax.ShapeDtypeStruct(out_shape, BF16),
        scratch_shapes=scratch,
        compiler_params=pltpu.CompilerParams(vmem_limit_bytes=VMEM_BYTES),
    )(*scalars, *arrays)


def exchange_kernel(amount, devices, *refs):
    sources, targets = refs[:amount], refs[amount : 2 * amount]
    send_sem, recv_sem, own_sem = refs[2 * amount :]
    me = lax.axis_index("tile")
    barrier = pltpu.get_barrier_semaphore()

    def greet(offset, _):
        peer = lax.rem(me + offset, devices)
        pl.semaphore_signal(
            barrier, inc=1, device_id={"tile": peer}, device_id_type=pl.DeviceIdType.MESH
        )
        return 0

    lax.fori_loop(1, devices, greet, 0)
    own = [
        pltpu.make_async_copy(source.at[me], target.at[me], own_sem.at[n])
        for n, (source, target) in enumerate(zip(sources, targets))
    ]
    for copy in own:
        copy.start()
    pl.semaphore_wait(barrier, devices - 1)

    def copies(offset):
        peer = lax.rem(me + offset, devices)
        return [
            pltpu.make_async_remote_copy(
                src_ref=source.at[peer],
                dst_ref=target.at[me],
                send_sem=send_sem.at[n, offset],
                recv_sem=recv_sem.at[n, offset],
                device_id={"tile": peer},
                device_id_type=pl.DeviceIdType.MESH,
            )
            for n, (source, target) in enumerate(zip(sources, targets))
        ]

    def begin(place, _):
        far = (place + 1) // 2
        for copy in copies(devices // 2 + far * (1 - 2 * lax.rem(place, 2))):
            copy.start()
        return 0

    def finish(offset, _):
        for copy in copies(offset):
            copy.wait()
        return 0

    lax.fori_loop(0, devices - 1, begin, 0)
    lax.fori_loop(1, devices, finish, 0)
    for copy in own:
        copy.wait()


def exchange(number, *arrays):
    amount, devices = len(arrays), arrays[0].shape[0]
    return pl.pallas_call(
        functools.partial(exchange_kernel, amount, devices),
        name=f"exchange{number}",
        in_specs=[pl.BlockSpec(memory_space=pl.ANY)] * amount,
        out_specs=[pl.BlockSpec(memory_space=pl.ANY)] * amount,
        out_shape=[jax.ShapeDtypeStruct(a.shape, a.dtype) for a in arrays],
        scratch_shapes=[
            pltpu.SemaphoreType.DMA((amount, devices)),
            pltpu.SemaphoreType.DMA((amount, devices)),
            pltpu.SemaphoreType.DMA((amount,)),
        ],
        compiler_params=pltpu.CompilerParams(collective_id=number, has_side_effects=True),
    )(*arrays)


def local(devices, pair_tiles, cotangent, w_pair, w_gate, w_out, tile_lists, list_counts):
    owned, side, _, channels = pair_tiles.shape
    cells = owned * side * side
    tiles, kmax = tile_lists.shape[1], tile_lists.shape[2]
    chans = channels // devices
    x = pair_tiles.reshape(2, side // 2, side, channels)
    cot = cotangent.reshape(x.shape)
    weights = w_pair.reshape(2, channels, 2, 2, devices, chans)
    weights = weights.transpose(0, 3, 4, 2, 5, 1).reshape(2, 2, 2 * channels, channels)
    wide = 2 * channels
    col, row = "c", "r"

    def lists(m):
        return tile_lists[m].reshape(-1), list_counts[m]

    folded = (side // 2, 2 * side)

    def triangle(lr, m):
        (lr,) = exchange(2 * m, lr.reshape(devices, 2 * chans, cells))
        lr = lr.reshape(tiles, 2, chans, *folded)
        kernel = functools.partial(triangle_kernel, m == 1, tiles, kmax, chans)
        prod = tile_call(kernel, f"triangle{m}", lists(m), (lr,), (tiles, chans, *folded), [])
        (prod,) = exchange(2 * m + 1, prod.reshape(tiles, chans, cells))
        return lr, prod.reshape(channels, cells)

    def triangle_back(lr, gprod, m, *others):
        (gprod,) = exchange(4 + 2 * m, gprod.reshape(devices, chans, cells))
        gprod = gprod.reshape(tiles, chans, *folded)
        kernel = functools.partial(triangle_back_kernel, m == 1, tiles, kmax, chans)
        sums = pltpu.VMEM((tiles, 2, chans, side, side), F32)
        glr = tile_call(kernel, f"triangle_back{m}", lists(m), (lr, gprod), lr.shape, [sums])
        glr, *others = exchange(5 + 2 * m, glr.reshape(tiles, 2 * chans, cells), *others)
        return glr.reshape(wide, cells), *others

    def by_rows(grad):
        return grad.astype(BF16).reshape(devices, channels // devices, -1)

    def whole(*arrays):
        return [("w", array) for array in arrays]

    low_cells = (col, (channels, cells), BF16)
    lr_cells = (col, (wide, cells), BF16)
    square = ("w", (channels, channels), F32)
    broad = ("w", (channels, 2 * wide), F32)
    rows_out = (row, x.shape, BF16)

    (lr0,) = cellwise(first_kernel, "first", [(row, x)] + whole(*weights[0]), [lr_cells], cells)
    lr0, prod0 = triangle(lr0, 0)
    pair1, lr1 = cellwise(
        middle_kernel, "middle",
        [(row, x), (col, prod0)] + whole(w_gate[0], w_out[0], *weights[1]),
        [low_cells, lr_cells], cells,
    )
    lr1, prod1 = triangle(lr1, 1)
    new_pair, gprod1, glogit1, dgate1, dout1 = cellwise(
        top_kernel, "top",
        [(col, pair1), (col, prod1), (row, cot)] + whole(w_gate[1], w_out[1]),
        [rows_out, low_cells, low_cells, square, square], cells,
    )
    (glr1,) = triangle_back(lr1, gprod1, 1)
    upstream, gprod0, glogit0, dpair1, dgate0, dout0 = cellwise(
        turn_kernel, "turn",
        [(row if a is cot or a is x else col, a) for a in (pair1, cot, glr1, glogit1, x, prod0)]
        + whole(*weights[1], w_gate[1], w_gate[0], w_out[0]),
        [(col, (channels, cells), F32), low_cells, low_cells, broad, square, square], cells,
    )
    early = jnp.concatenate([dpair1, dgate1, dout1, dgate0, dout0], axis=1)
    glr0, early = triangle_back(lr0, gprod0, 0, by_rows(early))
    d_pair, dpair0 = cellwise(
        last_kernel, "last",
        [(row, x), (col, upstream), (col, glr0), (col, glogit0)] + whole(*weights[0], w_gate[0]),
        [rows_out, broad], cells,
    )

    scale = 1.0 / math.sqrt(tiles * side * side)

    def unpermute(pair):
        pair = pair.reshape(-1, 2, devices, 2, chans).transpose(0, 3, 1, 2, 4)
        return pair.reshape(-1, 2 * wide)

    early = jnp.sum(early.astype(F32), axis=0) * scale
    late = jnp.sum(exchange(8, by_rows(dpair0))[0].astype(F32), axis=0) * scale
    ends = [2 * wide + channels * n for n in range(5)]
    dgate1, dout1, dgate0, dout0 = [early[:, a:b] for a, b in zip(ends, ends[1:])]
    return (
        new_pair.reshape(pair_tiles.shape),
        d_pair.reshape(pair_tiles.shape),
        jnp.stack([unpermute(late), unpermute(early[:, : 2 * wide])]),
        jnp.stack([dgate0, dgate1]),
        jnp.stack([dout0, dout1]),
    )


def solution(mesh):
    cells = P(("groups", "tile"), None, None, None)
    in_specs = (cells, cells, P(), P(), P(), P(None, "groups", None, None), P(None, "groups"))
    grads = P("groups", "tile", None)
    return jax.shard_map(
        functools.partial(local, mesh.shape["tile"]), mesh=mesh, in_specs=in_specs,
        out_specs=(cells, cells, grads, grads, grads), check_vma=False,
    )
```
